32 devices in a mesh: group: 2 (over x), brick: 16 (over z, y, core).
Axes of the slice: x: 2, y: 2, z: 4, core: 2. Of those that a mesh axis runs over, the one named last changes fastest.
Arguments:
- subjects: float32 [4, 128, 64, 256], P('group', 'brick'), parts along dimension 0, may hold values from -24 to 24
- template: float32 [256, 64, 256], P(('group', 'brick')), parts along dimension 0, may hold values from -8 to 8
Outputs:
- atlas: float32 [256, 64, 256], P(('group', 'brick')), parts along dimension 0
- fields: float32 [3, 4, 128, 64, 256], P(None, 'group', 'brick'), parts along dimension 1
The draws below stay inside these ranges and needn't reach their ends.
There are 2 independent parts, one for each index of `group`. The reference program is written for one: setup_inputs(seed, part) draws one part's arguments, and reference() takes and returns one part's arrays. A program takes and returns all parts, laid end to end along the dimension named above; each array names one. Nothing has to cross between parts.
All inputs are finite; a program needn't handle non-finite values.
Results may differ from the reference program's by a relative error of at most 0.0001.
Values sent between devices are 32-bit elements; how exact they have to be, the bound alone decides.
A program may use at most 64 MiB of HBM per device.

```python
import math
import jax
import jax.numpy as jnp
from jax import lax

S = 2
NB = 64
NC = 256
RAD = 2
ROUNDS = 2
ITERS = 3
NX = 128


def wave_sum(key, first, second, third, count, amp_lo, amp_hi, wave_lo, wave_hi):
    numbers = jax.random.uniform(jax.random.fold_in(key, 1), (count, 3), jnp.float32, wave_lo, wave_hi)
    signs = (jax.random.randint(jax.random.fold_in(key, 2), (count, 3), 0, 2) * 2 - 1).astype(jnp.float32)
    numbers = numbers * signs
    amplitude = jax.random.uniform(jax.random.fold_in(key, 3), (count,), jnp.float32, amp_lo, amp_hi)
    phases = jax.random.uniform(jax.random.fold_in(key, 4), (count,), jnp.float32, 0.0, 6.283185)
    total = jnp.zeros_like(first + second + third)
    for index in range(count):
        argument = numbers[index, 0] * first + numbers[index, 1] * second + numbers[index, 2] * third + phases[index]
        total = total + amplitude[index] * jnp.sin(argument)
    return total


def pattern_at(key, first, second, third):
    base = jax.random.fold_in(key, 101)
    return wave_sum(base, first, second, third, 6, 0.6, 1.0, 0.15, 0.45)


def draw_subjects(key, part):
    first = jnp.arange(NX, dtype=jnp.float32)[None, :, None, None]
    second = jnp.arange(NB, dtype=jnp.float32)[None, None, :, None]
    third = jnp.arange(NC, dtype=jnp.float32)[None, None, None, :]
    shift_key = jax.random.fold_in(key, 202)
    shift_waves = jax.random.uniform(jax.random.fold_in(shift_key, 1), (S, 3, 3), jnp.float32, 0.04, 0.12)
    shift_amps = jax.random.uniform(jax.random.fold_in(shift_key, 2), (S, 3), jnp.float32, 0.5, 1.0)
    shift_phase = jax.random.uniform(jax.random.fold_in(shift_key, 3), (S, 3), jnp.float32, 0.0, 6.283185)
    moved = []
    for comp in range(3):
        wave_first = shift_waves[:, comp, 0][:, None, None, None]
        wave_second = shift_waves[:, comp, 1][:, None, None, None]
        wave_third = shift_waves[:, comp, 2][:, None, None, None]
        phase_here = shift_phase[:, comp][:, None, None, None]
        amp_here = shift_amps[:, comp][:, None, None, None]
        moved.append(amp_here * jnp.sin(wave_first * first + wave_second * second + wave_third * third + phase_here))
    position = jnp.arange(NX, dtype=jnp.float32) / max(NX - 1, 1)
    scale = (1.0 + 2.0 * position)[None, :, None, None]
    noise_key = jax.random.fold_in(key, 303)
    pattern = pattern_at(key, first + moved[0], second + moved[1], third + moved[2])
    noise = 0.3 * jnp.clip(jax.random.normal(noise_key, (S, NX, NB, NC), jnp.float32), -3.0, 3.0)
    return (pattern + noise) * scale


def draw_template(key, part):
    first = jnp.arange(NX, dtype=jnp.float32)[:, None, None]
    second = jnp.arange(NB, dtype=jnp.float32)[None, :, None]
    third = jnp.arange(NC, dtype=jnp.float32)[None, None, :]
    noise_key = jax.random.fold_in(key, 404)
    pattern = pattern_at(key, first, second, third)
    noise = 0.3 * jnp.clip(jax.random.normal(noise_key, (NX, NB, NC), jnp.float32), -3.0, 3.0)
    return pattern + noise


def setup_inputs(seed: int = 0, part: int = 0) -> dict:
    splits = jax.random.split(jax.random.key(seed), 3)
    own_keys = jax.random.split(jax.random.fold_in(splits[2], part), 3)
    subjects = draw_subjects(jax.random.fold_in(jax.random.fold_in(splits[2], part), 71), part)
    template = draw_template(jax.random.fold_in(jax.random.fold_in(splits[2], part), 71), part)
    return dict(subjects=subjects, template=template)


SIGMA = 1.5
STEP = 1.0
KAPPA = 0.5
EPS = 1e-05

def taps_list(radius):
    raw = [math.exp(-(k * k) / (2.0 * SIGMA * SIGMA)) for k in range(-radius, radius + 1)]
    total = 0.0
    for value in raw:
        total = total + value
    return [value / total for value in raw]

def hat(value):
    return jnp.maximum(0.0, 1.0 - jnp.abs(value))

def pad_last(volume):
    return jnp.pad(volume, [(0, 0)] * (volume.ndim - 2) + [(1, 1), (1, 1)])

def warp_image(padded, disp):
    planes, rows, cols = (disp.shape[2], disp.shape[3], disp.shape[4])
    first_w = [hat(disp[0] - a) for a in (-1, 0, 1)]
    second_w = [hat(disp[1] - b) for b in (-1, 0, 1)]
    third_w = [hat(disp[2] - c) for c in (-1, 0, 1)]
    result = jnp.zeros(disp.shape[1:], jnp.float32)
    for ia, a in enumerate((-1, 0, 1)):
        inner = jnp.zeros(disp.shape[1:], jnp.float32)
        for ib, b in enumerate((-1, 0, 1)):
            line = jnp.zeros(disp.shape[1:], jnp.float32)
            for ic, c in enumerate((-1, 0, 1)):
                piece = padded[:, 1 + a:1 + a + planes, 1 + b:1 + b + rows, 1 + c:1 + c + cols]
                line = line + third_w[ic] * piece
            inner = inner + second_w[ib] * line
        result = result + first_w[ia] * inner
    return result

def gradient(tpad):
    g_first = (tpad[2:, 1:-1, 1:-1] - tpad[:-2, 1:-1, 1:-1]) * 0.5
    g_second = (tpad[1:-1, 2:, 1:-1] - tpad[1:-1, :-2, 1:-1]) * 0.5
    g_third = (tpad[1:-1, 1:-1, 2:] - tpad[1:-1, 1:-1, :-2]) * 0.5
    return jnp.stack([g_first, g_second, g_third])

def forces(state, warped, current, grads):
    diff = current[None] - warped
    denom = (grads[0] * grads[0] + grads[1] * grads[1] + grads[2] * grads[2])[None] + diff * diff + KAPPA
    ratio = STEP * diff / denom
    return state + grads[:, None] * ratio[None]

def first_pass(extended, planes):
    taps = taps_list(RAD)
    result = taps[0] * lax.slice_in_dim(extended, 0, planes, axis=2)
    for k in range(1, 2 * RAD + 1):
        result = result + taps[k] * lax.slice_in_dim(extended, k, k + planes, axis=2)
    return result

def along_axis(volume, axis):
    taps = taps_list(RAD)
    size_here = volume.shape[axis]
    pads = [(0, 0)] * volume.ndim
    pads[axis] = (RAD, RAD)
    padded = jnp.pad(volume, pads)
    result = taps[0] * lax.slice_in_dim(padded, 0, size_here, axis=axis)
    for k in range(1, 2 * RAD + 1):
        result = result + taps[k] * lax.slice_in_dim(padded, k, k + size_here, axis=axis)
    return result

def normalize(mean_image):
    count = mean_image.shape[0] * mean_image.shape[1] * mean_image.shape[2]
    mu = jnp.sum(mean_image) / count
    centered = mean_image - mu
    var = jnp.sum(centered * centered) / count
    return centered / jnp.sqrt(var + EPS)

def reference(subjects, template):
    fields = jnp.zeros((3,) + subjects.shape, jnp.float32)
    image_pad = jnp.pad(subjects, ((0, 0), (1, 1), (1, 1), (1, 1)))
    current = template
    for rnd in range(ROUNDS):
        grads = gradient(jnp.pad(current, 1))
        for step in range(ITERS):
            warped = warp_image(image_pad, jnp.tanh(fields))
            update = forces(fields, warped, current, grads)
            wide = jnp.pad(update, ((0, 0), (0, 0), (RAD, RAD), (0, 0), (0, 0)))
            fields = along_axis(along_axis(first_pass(wide, update.shape[2]), 3), 4)
        warped = warp_image(image_pad, jnp.tanh(fields))
        current = normalize(lax.optimization_barrier(jnp.mean(warped, axis=0)))
    return (current, fields)
```

```python
import math

import jax
import jax.numpy as jnp
from jax import lax
from jax.experimental import pallas as pl
from jax.experimental.pallas import tpu as pltpu
from jax.sharding import PartitionSpec as P

RAD = 2
ROUNDS = 2
ITERS = 3


SIGMA = 1.5
STEP = 1.0
KAPPA = 0.5
EPS = 1e-05


def padded_2(shard, sides, width):
    for axis, dim in sides:
        count, length = (lax.axis_size(axis), shard.shape[dim])
        up = [(i, (i + 1) % count) for i in range(count - 1)]
        down = [(j, i) for i, j in up]
        last = lax.slice_in_dim(shard, length - width, length, axis=dim)
        initial = lax.slice_in_dim(shard, 0, width, axis=dim)
        before = lax.ppermute(last, axis, up)
        after = lax.ppermute(initial, axis, down)
        shard = jnp.concatenate([before, shard, after], axis=dim)
    return shard


def taps_list(radius):
    raw = [math.exp(-(k * k) / (2.0 * SIGMA * SIGMA)) for k in range(-radius, radius + 1)]
    total = 0.0
    for value in raw:
        total = total + value
    return [value / total for value in raw]


def hat(value):
    return jnp.maximum(0.0, 1.0 - jnp.abs(value))


def pad_last(volume):
    return jnp.pad(volume, [(0, 0)] * (volume.ndim - 2) + [(1, 1), (1, 1)])


def warp_image(padded, disp):
    planes, rows, cols = (disp.shape[2], disp.shape[3], disp.shape[4])
    first_w = [hat(disp[0] - a) for a in (-1, 0, 1)]
    second_w = [hat(disp[1] - b) for b in (-1, 0, 1)]
    third_w = [hat(disp[2] - c) for c in (-1, 0, 1)]
    result = jnp.zeros(disp.shape[1:], jnp.float32)
    for ia, a in enumerate((-1, 0, 1)):
        inner = jnp.zeros(disp.shape[1:], jnp.float32)
        for ib, b in enumerate((-1, 0, 1)):
            line = jnp.zeros(disp.shape[1:], jnp.float32)
            for ic, c in enumerate((-1, 0, 1)):
                piece = padded[
                    :, 1 + a : 1 + a + planes, 1 + b : 1 + b + rows, 1 + c : 1 + c + cols
                ]
                line = line + third_w[ic] * piece
            inner = inner + second_w[ib] * line
        result = result + first_w[ia] * inner
    return result


def gradient(tpad):
    g_first = (tpad[2:, 1:-1, 1:-1] - tpad[:-2, 1:-1, 1:-1]) * 0.5
    g_second = (tpad[1:-1, 2:, 1:-1] - tpad[1:-1, :-2, 1:-1]) * 0.5
    g_third = (tpad[1:-1, 1:-1, 2:] - tpad[1:-1, 1:-1, :-2]) * 0.5
    return jnp.stack([g_first, g_second, g_third])


def forces(state, warped, current, grads):
    diff = current[None] - warped
    denom = (
        (grads[0] * grads[0] + grads[1] * grads[1] + grads[2] * grads[2])[None]
        + diff * diff
        + KAPPA
    )
    ratio = STEP * diff / denom
    return state + grads[:, None] * ratio[None]


def first_pass(extended, planes):
    taps = taps_list(RAD)
    result = taps[0] * lax.slice_in_dim(extended, 0, planes, axis=2)
    for k in range(1, 2 * RAD + 1):
        result = result + taps[k] * lax.slice_in_dim(extended, k, k + planes, axis=2)
    return result


def along_axis(volume, axis):
    taps = taps_list(RAD)
    size_here = volume.shape[axis]
    pads = [(0, 0)] * volume.ndim
    pads[axis] = (RAD, RAD)
    padded = jnp.pad(volume, pads)
    result = taps[0] * lax.slice_in_dim(padded, 0, size_here, axis=axis)
    for k in range(1, 2 * RAD + 1):
        result = result + taps[k] * lax.slice_in_dim(padded, k, k + size_here, axis=axis)
    return result


def gather_kernel(n, x_ref, o_ref, send_sem, recv_sem):
    me = lax.axis_index("brick")
    barrier = pltpu.get_barrier_semaphore()
    for k in range(1, n):
        pl.semaphore_signal(
            barrier, inc=1, device_id={"brick": lax.rem(me + k, n)},
            device_id_type=pl.DeviceIdType.MESH,
        )
    pl.semaphore_wait(barrier, n - 1)
    copies = []
    for k in range(1, n):
        copy = pltpu.make_async_remote_copy(
            src_ref=x_ref,
            dst_ref=o_ref.at[k],
            send_sem=send_sem.at[k],
            recv_sem=recv_sem.at[k],
            device_id={"brick": lax.rem(me + k, n)},
            device_id_type=pl.DeviceIdType.MESH,
        )
        copy.start()
        copies.append(copy)
    o_ref[0] = x_ref[...]
    for copy in copies:
        copy.wait()


def gather_tiles(tile, n):
    return pl.pallas_call(
        lambda *refs: gather_kernel(n, *refs),
        out_shape=jax.ShapeDtypeStruct((n,) + tile.shape, tile.dtype),
        in_specs=[pl.BlockSpec(memory_space=pltpu.VMEM)],
        out_specs=pl.BlockSpec(memory_space=pltpu.VMEM),
        scratch_shapes=[pltpu.SemaphoreType.DMA((n,)), pltpu.SemaphoreType.DMA((n,))],
        compiler_params=pltpu.CompilerParams(collective_id=0, has_side_effects=True),
    )(tile)


def normalize(mean_image, count):
    n = lax.axis_size("brick")
    own = count // n
    total = jnp.sum(mean_image)
    away = mean_image - total / own
    spread = jnp.sum(away * away)
    lane = lax.broadcasted_iota(jnp.int32, (8, 128), 1)
    tile = jnp.where(lane == 0, total, jnp.where(lane == 1, spread, 0.0))
    every = gather_tiles(tile, n)
    totals, spreads = every[:, 0, 0], every[:, 0, 1]
    mu = jnp.sum(totals) / count
    offsets = totals / own - mu
    var = (jnp.sum(spreads) + own * jnp.sum(offsets * offsets)) / count
    return (mean_image - mu) / jnp.sqrt(var + EPS)


def per_device(subjects, template):
    planes = subjects.shape[1]
    total_planes = planes * lax.axis_size("brick")
    count = total_planes * subjects.shape[2] * subjects.shape[3]
    fields = jnp.zeros((3,) + subjects.shape, jnp.float32)
    current = template
    image_pad = pad_last(padded_2(subjects, (("brick", 1),), 1))
    for rnd in range(ROUNDS):
        tpad = pad_last(padded_2(current, (("brick", 0),), 1))
        grads = gradient(tpad)
        for step in range(ITERS):
            warped = warp_image(image_pad, jnp.tanh(fields))
            update = forces(fields, warped, current, grads)
            wide = padded_2(update, (("brick", 2),), RAD)
            fields = along_axis(along_axis(first_pass(wide, planes), 3), 4)
        warped = warp_image(image_pad, jnp.tanh(fields))
        current = normalize(jnp.mean(warped, axis=0), count)
    return (current, fields)


def solution(mesh):
    return jax.shard_map(
        per_device,
        mesh=mesh,
        in_specs=(P("group", "brick", None, None), P(("group", "brick"), None, None)),
        out_specs=(P(("group", "brick"), None, None), P(None, "group", "brick", None, None)),
        check_vma=False,
    )
```

```python
import math

import jax
import jax.numpy as jnp
import ml_dtypes
import numpy as np
from jax import lax
from jax.experimental import pallas as pl
from jax.experimental.pallas import tpu as pltpu
from jax.sharding import PartitionSpec as P

RAD = 2
ROUNDS = 2
ITERS = 3

SIGMA = 1.5
STEP = 1.0
KAPPA = 0.5
EPS = 1e-05

LOCAL = 1
HS = max(1, RAD * LOCAL)
HT = HS + 1
HU = max(RAD, RAD * LOCAL)
HF = HU - RAD

MESH = pl.DeviceIdType.MESH


def taps_list(radius):
    raw = [math.exp(-(k * k) / (2.0 * SIGMA * SIGMA)) for k in range(-radius, radius + 1)]
    total = 0.0
    for value in raw:
        total = total + value
    return [value / total for value in raw]


def band(size):
    taps = taps_list(RAD)
    full = np.zeros((size, size), np.float64)
    for k in range(-RAD, RAD + 1):
        full += np.diag(np.full(size - abs(k), taps[k + RAD]), k)
    high = full.astype(np.float32).astype(ml_dtypes.bfloat16)
    low = (full - high.astype(np.float64)).astype(np.float32).astype(ml_dtypes.bfloat16)
    return high, low


def split(value):
    high = value.astype(jnp.bfloat16)
    low = (value - high.astype(jnp.float32)).astype(jnp.bfloat16)
    return high, low


def moved(value, axis, step):
    if step == 0:
        return value
    size = value.shape[axis]
    index = lax.broadcasted_iota(jnp.int32, value.shape, axis)
    edge = size - 1 if step > 0 else 0
    return jnp.where(index == edge, 0.0, pltpu.roll(value, (-step) % size, axis))


def kernel(n, subjects, template, wrow, wcol, atlas, fields_out,
           images, cur, grad, upd, fld, warped, mean, half_hi, half_lo, stats, tile,
           load_sem, in_send, in_recv, upd_send, upd_recv, mean_send, mean_recv,
           stat_send, stat_recv, out_sem):
    me = lax.axis_index("brick")
    count_s, planes, rows, cols = subjects.shape
    has_low, has_high = me > 0, me < n - 1
    first, last = me == 0, me == n - 1
    low, high = {"brick": me - 1}, {"brick": me + 1}
    total_planes = n * planes
    taps = taps_list(RAD)

    barrier = pltpu.get_barrier_semaphore()
    for k in range(1, n):
        pl.semaphore_signal(barrier, inc=1, device_id={"brick": lax.rem(me + k, n)}, device_id_type=MESH)
    pl.semaphore_wait(barrier, n - 1)

    def inside(p):
        place = me * planes + p
        return jnp.logical_and(place >= 0, place < total_planes)

    def faces(src, dst, halo, base_src, base_dst, lead, send, recv):
        up = pltpu.make_async_remote_copy(
            src_ref=src.at[lead + (pl.ds(base_src + planes - halo, halo),)],
            dst_ref=dst.at[lead + (pl.ds(base_dst - halo, halo),)],
            send_sem=send.at[0], recv_sem=recv.at[0], device_id=high, device_id_type=MESH)
        down = pltpu.make_async_remote_copy(
            src_ref=src.at[lead + (pl.ds(base_src, halo),)],
            dst_ref=dst.at[lead + (pl.ds(base_dst + planes, halo),)],
            send_sem=send.at[1], recv_sem=recv.at[1], device_id=low, device_id_type=MESH)
        return up, down

    def start(pair):
        pl.when(has_high)(lambda: pair[0].start())
        pl.when(has_low)(lambda: pair[1].start())

    def finish(pair):
        @pl.when(has_high)
        def _():
            pair[0].wait_send()
            pair[1].wait_recv()

        @pl.when(has_low)
        def _():
            pair[1].wait_send()
            pair[0].wait_recv()

    own = images.at[4]
    whole = slice(None)
    sub_pair = faces(subjects, own, HS, 0, HS, (whole,), in_send.at[0], in_recv.at[0])
    tem_pair = faces(template, cur, HT, 0, HT, (), in_send.at[1], in_recv.at[1])
    start(tem_pair)
    start(sub_pair)
    load_s = pltpu.make_async_copy(subjects, own.at[:, pl.ds(HS, planes)], load_sem.at[0])
    load_t = pltpu.make_async_copy(template, cur.at[pl.ds(HT, planes)], load_sem.at[1])
    load_s.start()
    load_t.start()

    def clear(ref, lead, halo, base):
        shape = (halo, rows, cols)

        @pl.when(first)
        def _():
            ref[lead + (pl.ds(base - halo, halo),)] = jnp.zeros(shape, jnp.float32)

        @pl.when(last)
        def _():
            ref[lead + (pl.ds(base + planes, halo),)] = jnp.zeros(shape, jnp.float32)

    clear(cur, (), HT, HT)
    for s in range(count_s):
        clear(images, (4, s), HS, HS)
        for slot in range(2):
            for k in range(3):
                clear(upd, (slot, s, k), HU, HU)

    def shift_planes(s, lo, hi):
        @pl.loop(lo + HS, hi + HS)
        def _(p):
            value = images[4, s, p]
            for c in (-1, 0, 1):
                side = moved(value, 1, c)
                for b in (-1, 0, 1):
                    if (b, c) != (0, 0):
                        images[(b + 1) * 3 + c + 1, s, p] = moved(side, 0, b)

    def gradients(lo, hi):
        @pl.loop(lo, hi)
        def _(p):
            here = cur[p + HT]
            g0 = (cur[p + HT + 1] - cur[p + HT - 1]) * 0.5
            g1 = (moved(here, 0, 1) - moved(here, 0, -1)) * 0.5
            g2 = (moved(here, 1, 1) - moved(here, 1, -1)) * 0.5
            grad[0, p + HU] = g0
            grad[1, p + HU] = g1
            grad[2, p + HU] = g2
            grad[3, p + HU] = g0 * g0 + g1 * g1 + g2 * g2 + KAPPA

    def chunks(lo, hi, body):
        per = rows // 8

        @pl.loop(0, (hi - lo) * per, unroll=2)
        def _(i):
            body(lo + i // per, pl.ds(pl.multiple_of((i % per) * 8, 8), 8))

    def warp(s, p, rs):
        u = [jnp.tanh(fld[s, k, p + HF, rs]) for k in range(3)]
        pos = [v > 0.0 for v in u]
        size = [jnp.abs(v) for v in u]

        def two(c):
            here, side = [], []
            for b in (0, 1, 2):
                where = b * 3 + c
                here.append(images[where, s, p + HS, rs])
                side.append(jnp.where(pos[0], images[where, s, p + HS + 1, rs], images[where, s, p + HS - 1, rs]))
            return (here[1], side[1], jnp.where(pos[1], here[2], here[0]), jnp.where(pos[1], side[2], side[0]))

        left, middle, right = two(0), two(1), two(2)
        beside = [jnp.where(pos[2], r, l) for r, l in zip(right, left)]
        lines = [m + size[2] * (o - m) for m, o in zip(middle, beside)]
        near = lines[0] + size[0] * (lines[1] - lines[0])
        far = lines[2] + size[0] * (lines[3] - lines[2])
        return near + size[1] * (far - near)

    def force(s, slot, lo, hi, kind):
        def body(p, rs):
            if kind == "subject":
                image = images[4, s, p + HS, rs]
            elif kind == "stored":
                image = warped[s, p, rs]
            else:
                image = warp(s, p, rs)
            diff = cur[p + HT, rs] - image
            ratio = STEP * diff / (grad[3, p + HU, rs] + diff * diff)
            for k in range(3):
                value = grad[k, p + HU, rs] * ratio
                if kind != "subject":
                    value = value + fld[s, k, p + HF, rs]
                if lo < 0:
                    value = jnp.where(inside(p), value, 0.0)
                upd[slot, s, k, p + HU, rs] = value

        chunks(lo, hi, body)

    def smooth(s, slot, lo, hi):
        number = hi - lo

        @pl.loop(0, 3)
        def _(k):
            @pl.loop(0, number)
            def _(i):
                at = i + lo + HU
                value = taps[2] * upd[slot, s, k, at]
                value = value + taps[1] * (upd[slot, s, k, at - 1] + upd[slot, s, k, at + 1])
                value = value + taps[0] * (upd[slot, s, k, at - 2] + upd[slot, s, k, at + 2])
                hi_part, lo_part = split(value)
                stack = jnp.concatenate([hi_part, lo_part, hi_part], axis=0)
                value = jnp.dot(wrow[...], stack, preferred_element_type=jnp.float32)
                hi_part, lo_part = split(value)
                half_hi[i] = hi_part
                half_lo[i] = lo_part

            a = half_hi[0:number].reshape(number * rows, cols)
            b = half_lo[0:number].reshape(number * rows, cols)
            stack = jnp.concatenate([a, b, a], axis=1)
            value = jnp.dot(stack, wcol[...], preferred_element_type=jnp.float32)
            fld[s, k, pl.ds(lo + HF, number)] = value.reshape(number, rows, cols)

    def exchange(s, slot):
        return faces(upd.at[slot, s], upd.at[slot, s], RAD, HU, HU, (whole,),
                     upd_send.at[slot, s], upd_recv.at[slot, s])

    def mean_image(keep):
        def body(p, rs):
            images_here = [warp(s, p, rs) for s in range(count_s)]
            if keep:
                for s in range(count_s):
                    warped[s, p, rs] = images_here[s]
            total = images_here[0]
            for value in images_here[1:]:
                total = total + value
            mean[p + 1, rs] = total * (1.0 / count_s)

        chunks(0, planes, body)

    def statistics(rnd, own_count):
        def add(p, total):
            return total + mean[p + 1]

        total = jnp.sum(lax.fori_loop(0, planes, add, jnp.zeros((rows, cols), jnp.float32)))
        center = total / own_count

        def square(p, total):
            away = mean[p + 1] - center
            return total + away * away

        spread = jnp.sum(lax.fori_loop(0, planes, square, jnp.zeros((rows, cols), jnp.float32)))
        lane = lax.broadcasted_iota(jnp.int32, (8, 128), 1)
        tile[rnd] = jnp.where(lane == 0, total, jnp.where(lane == 1, spread, 0.0))
        stats[rnd, 0] = tile[rnd]
        copies = []
        for k in range(1, n):
            copy = pltpu.make_async_remote_copy(
                src_ref=tile.at[rnd], dst_ref=stats.at[rnd, k],
                send_sem=stat_send.at[rnd, k], recv_sem=stat_recv.at[rnd, k],
                device_id={"brick": lax.rem(me + k, n)}, device_id_type=MESH)
            copy.start()
            copies.append(copy)
        for copy in copies:
            copy.wait()
        every = stats[rnd]
        lanes = lax.broadcasted_iota(jnp.int32, (n, 8, 128), 2)
        rows_of = lax.broadcasted_iota(jnp.int32, (n, 8, 128), 1)
        on_sum = jnp.logical_and(lanes == 0, rows_of == 0)
        on_spread = jnp.logical_and(lanes == 1, rows_of == 0)
        count = own_count * n
        mu = jnp.sum(jnp.where(on_sum, every, 0.0)) / count
        offsets = jnp.where(on_sum, every / own_count - mu, 0.0)
        var = (jnp.sum(jnp.where(on_spread, every, 0.0)) + own_count * jnp.sum(offsets * offsets)) / count
        scale = 1.0 / jnp.sqrt(jnp.full((8, cols), var + EPS, jnp.float32))
        return mu, scale

    own_count = float(planes * rows * cols)
    out_copies = []

    load_s.wait()
    for s in range(count_s):
        shift_planes(s, 0, planes)
    load_t.wait()
    finish(tem_pair)
    gradients(-HU if LOCAL else 0, planes + (HU if LOCAL else 0))
    finish(sub_pair)
    reach = HF + 1
    for s in range(count_s):
        shift_planes(s, -reach, 0)
        shift_planes(s, planes, planes + reach)

    pairs = {}
    for rnd in range(ROUNDS):
        for step in range(ITERS):
            slot = (rnd * ITERS + step) % 2
            local = rnd == 0 and step < LOCAL
            wide = RAD * (LOCAL - step) if local else 0
            kind = "warp" if step else ("stored" if rnd else "subject")
            for s in range(count_s):
                if step:
                    settle(s)
                force(s, slot, -wide, planes + wide, kind)
                if not local:
                    pairs[s] = exchange(s, slot)
                    start(pairs[s])

            def settle(s, slot=slot, local=local, wide=wide):
                if not local:
                    finish(pairs[s])
                grow = wide - RAD if local else 0
                smooth(s, slot, -grow, planes + grow)
        for s in range(count_s):
            settle(s)
            if rnd == ROUNDS - 1:
                for k in range(3):
                    copy = pltpu.make_async_copy(
                        fld.at[s, k, pl.ds(HF, planes)], fields_out.at[k, s], out_sem.at[s, k])
                    copy.start()
                    out_copies.append(copy)
        mean_image(rnd < ROUNDS - 1)
        more = rnd < ROUNDS - 1
        if more:
            pair = faces(mean, mean, 1, 1, 1, (), mean_send, mean_recv)
            start(pair)
        mu, scale = statistics(rnd, own_count)
        if more:
            finish(pair)
        reach_mean = 1 if more else 0

        def normal(p, rs):
            value = (mean[p + 1, rs] - mu) * scale
            if more:
                value = jnp.where(inside(p), value, 0.0)
            cur[p + HT, rs] = value

        if more:
            clear(mean, (), 1, 1)
        chunks(-reach_mean, planes + reach_mean, normal)
        if more:
            gradients(0, planes)
    copy = pltpu.make_async_copy(cur.at[pl.ds(HT, planes)], atlas, load_sem.at[1])
    copy.start()
    for other in out_copies:
        other.wait()
    copy.wait()


def per_device(subjects, template):
    n = lax.axis_size("brick")
    count_s, planes, rows, cols = subjects.shape
    row_hi, row_lo = band(rows)
    col_hi, col_lo = band(cols)
    wrow = jnp.asarray(np.concatenate([row_hi, row_hi, row_lo], axis=1))
    wcol = jnp.asarray(np.concatenate([col_hi, col_hi, col_lo], axis=0))
    anywhere = pl.BlockSpec(memory_space=pl.ANY)
    in_vmem = pl.BlockSpec(memory_space=pltpu.VMEM)
    dma = pltpu.SemaphoreType.DMA
    f32 = jnp.float32
    face = (rows, cols)
    atlas, fields = pl.pallas_call(
        lambda *refs: kernel(n, *refs),
        out_shape=(jax.ShapeDtypeStruct(template.shape, f32), jax.ShapeDtypeStruct((3,) + subjects.shape, f32)),
        in_specs=[anywhere, anywhere, in_vmem, in_vmem],
        out_specs=(anywhere, anywhere),
        scratch_shapes=[
            pltpu.VMEM((9, count_s, planes + 2 * HS) + face, f32),
            pltpu.VMEM((planes + 2 * HT,) + face, f32),
            pltpu.VMEM((4, planes + 2 * HU) + face, f32),
            pltpu.VMEM((2, count_s, 3, planes + 2 * HU) + face, f32),
            pltpu.VMEM((count_s, 3, planes + 2 * HF) + face, f32),
            pltpu.VMEM((count_s, planes) + face, f32),
            pltpu.VMEM((planes + 2,) + face, f32),
            pltpu.VMEM((planes + 2 * HF,) + face, jnp.bfloat16),
            pltpu.VMEM((planes + 2 * HF,) + face, jnp.bfloat16),
            pltpu.VMEM((ROUNDS, n, 8, 128), f32),
            pltpu.VMEM((ROUNDS, 8, 128), f32),
            dma((2,)),
            dma((2, 2)), dma((2, 2)),
            dma((2, count_s, 2)), dma((2, count_s, 2)),
            dma((2,)), dma((2,)),
            dma((ROUNDS, n)), dma((ROUNDS, n)),
            dma((count_s, 3)),
        ],
        compiler_params=pltpu.CompilerParams(
            collective_id=0, has_side_effects=True, vmem_limit_bytes=60 * 1024 * 1024),
    )(subjects, template, wrow, wcol)
    return atlas, fields


def solution(mesh):
    return jax.shard_map(
        per_device,
        mesh=mesh,
        in_specs=(P("group", "brick", None, None), P(("group", "brick"), None, None)),
        out_specs=(P(("group", "brick"), None, None), P(None, "group", "brick", None, None)),
        check_vma=False,
    )
```

```python
import math

import jax
import jax.numpy as jnp
import ml_dtypes
import numpy as np
from jax import lax
from jax.experimental import pallas as pl
from jax.experimental.pallas import tpu as pltpu
from jax.sharding import PartitionSpec as P

RAD = 2
ROUNDS = 2
ITERS = 3

SIGMA = 1.5
STEP = 1.0
KAPPA = 0.5
EPS = 1e-05

LOCAL = 1
HS = max(1, RAD * LOCAL)
HT = HS + 1
HU = max(RAD, RAD * LOCAL)
HF = HU - RAD

MESH = pl.DeviceIdType.MESH


def taps_list(radius):
    raw = [math.exp(-(k * k) / (2.0 * SIGMA * SIGMA)) for k in range(-radius, radius + 1)]
    total = 0.0
    for value in raw:
        total = total + value
    return [value / total for value in raw]


def band(size):
    taps = taps_list(RAD)
    full = np.zeros((size, size), np.float64)
    for k in range(-RAD, RAD + 1):
        full += np.diag(np.full(size - abs(k), taps[k + RAD]), k)
    high = full.astype(np.float32).astype(ml_dtypes.bfloat16)
    low = (full - high.astype(np.float64)).astype(np.float32).astype(ml_dtypes.bfloat16)
    return high, low


def split(value):
    high = value.astype(jnp.bfloat16)
    low = (value - high.astype(jnp.float32)).astype(jnp.bfloat16)
    return high, low


def moved(value, axis, step):
    if step == 0:
        return value
    size = value.shape[axis]
    index = lax.broadcasted_iota(jnp.int32, value.shape, axis)
    edge = size - 1 if step > 0 else 0
    return jnp.where(index == edge, 0.0, pltpu.roll(value, (-step) % size, axis))


def kernel(n, subjects, template, wrow, wcol, atlas, fields_out,
           images, cur, grad, upd, fld, warped, mean, half_hi, half_lo, stats, tile,
           load_sem, in_send, in_recv, upd_send, upd_recv, mean_send, mean_recv,
           stat_send, stat_recv, out_sem):
    me = lax.axis_index("brick")
    count_s, planes, rows, cols = subjects.shape
    has_low, has_high = me > 0, me < n - 1
    first, last = me == 0, me == n - 1
    low, high = {"brick": me - 1}, {"brick": me + 1}
    total_planes = n * planes
    taps = taps_list(RAD)

    barrier = pltpu.get_barrier_semaphore()
    for k in range(1, n):
        pl.semaphore_signal(barrier, inc=1, device_id={"brick": lax.rem(me + k, n)}, device_id_type=MESH)
    pl.semaphore_wait(barrier, n - 1)

    def inside(p):
        place = me * planes + p
        return jnp.logical_and(place >= 0, place < total_planes)

    def faces(src, dst, halo, base_src, base_dst, lead, send, recv):
        up = pltpu.make_async_remote_copy(
            src_ref=src.at[lead + (pl.ds(base_src + planes - halo, halo),)],
            dst_ref=dst.at[lead + (pl.ds(base_dst - halo, halo),)],
            send_sem=send.at[0], recv_sem=recv.at[0], device_id=high, device_id_type=MESH)
        down = pltpu.make_async_remote_copy(
            src_ref=src.at[lead + (pl.ds(base_src, halo),)],
            dst_ref=dst.at[lead + (pl.ds(base_dst + planes, halo),)],
            send_sem=send.at[1], recv_sem=recv.at[1], device_id=low, device_id_type=MESH)
        return up, down

    def start(pair):
        pl.when(has_high)(lambda: pair[0].start())
        pl.when(has_low)(lambda: pair[1].start())

    def finish(pair):
        @pl.when(has_high)
        def _():
            pair[0].wait_send()
            pair[1].wait_recv()

        @pl.when(has_low)
        def _():
            pair[1].wait_send()
            pair[0].wait_recv()

    own = images.at[4]
    whole = slice(None)
    sub_pair = faces(subjects, own, HS, 0, HS, (whole,), in_send.at[0], in_recv.at[0])
    tem_pair = faces(template, cur, HT, 0, HT, (), in_send.at[1], in_recv.at[1])
    start(tem_pair)
    start(sub_pair)
    load_s = pltpu.make_async_copy(subjects, own.at[:, pl.ds(HS, planes)], load_sem.at[0])
    load_t = pltpu.make_async_copy(template, cur.at[pl.ds(HT, planes)], load_sem.at[1])
    load_s.start()
    load_t.start()

    def clear(ref, lead, halo, base):
        shape = (halo, rows, cols)

        @pl.when(first)
        def _():
            ref[lead + (pl.ds(base - halo, halo),)] = jnp.zeros(shape, jnp.float32)

        @pl.when(last)
        def _():
            ref[lead + (pl.ds(base + planes, halo),)] = jnp.zeros(shape, jnp.float32)

    clear(cur, (), HT, HT)
    for s in range(count_s):
        clear(images, (4, s), HS, HS)
        for slot in range(2):
            for k in range(3):
                clear(upd, (slot, s, k), HU, HU)

    def shift_planes(s, lo, hi):
        @pl.loop(lo + HS, hi + HS)
        def _(p):
            value = images[4, s, p]
            for c in (-1, 0, 1):
                side = moved(value, 1, c)
                for b in (-1, 0, 1):
                    if (b, c) != (0, 0):
                        images[(b + 1) * 3 + c + 1, s, p] = moved(side, 0, b)

    def gradients(lo, hi):
        @pl.loop(lo, hi)
        def _(p):
            here = cur[p + HT]
            g0 = (cur[p + HT + 1] - cur[p + HT - 1]) * 0.5
            g1 = (moved(here, 0, 1) - moved(here, 0, -1)) * 0.5
            g2 = (moved(here, 1, 1) - moved(here, 1, -1)) * 0.5
            grad[0, p + HU] = g0
            grad[1, p + HU] = g1
            grad[2, p + HU] = g2
            grad[3, p + HU] = g0 * g0 + g1 * g1 + g2 * g2 + KAPPA

    def chunks(lo, hi, body):
        per = rows // 8

        @pl.loop(0, (hi - lo) * per, unroll=2)
        def _(i):
            body(lo + i // per, pl.ds(pl.multiple_of((i % per) * 8, 8), 8))

    def warp(s, p, rs):
        u = [jnp.tanh(fld[s, k, p + HF, rs]) for k in range(3)]
        pos = [v > 0.0 for v in u]
        size = [jnp.abs(v) for v in u]

        def two(c):
            here, side = [], []
            for b in (0, 1, 2):
                where = b * 3 + c
                here.append(images[where, s, p + HS, rs])
                side.append(jnp.where(pos[0], images[where, s, p + HS + 1, rs], images[where, s, p + HS - 1, rs]))
            return (here[1], side[1], jnp.where(pos[1], here[2], here[0]), jnp.where(pos[1], side[2], side[0]))

        left, middle, right = two(0), two(1), two(2)
        beside = [jnp.where(pos[2], r, l) for r, l in zip(right, left)]
        lines = [m + size[2] * (o - m) for m, o in zip(middle, beside)]
        near = lines[0] + size[0] * (lines[1] - lines[0])
        far = lines[2] + size[0] * (lines[3] - lines[2])
        return near + size[1] * (far - near)

    def force(s, slot, lo, hi, kind):
        def body(p, rs):
            if kind == "subject":
                image = images[4, s, p + HS, rs]
            elif kind == "stored":
                image = warped[s, p, rs]
            else:
                image = warp(s, p, rs)
            diff = cur[p + HT, rs] - image
            ratio = STEP * diff / (grad[3, p + HU, rs] + diff * diff)
            for k in range(3):
                value = grad[k, p + HU, rs] * ratio
                if kind != "subject":
                    value = value + fld[s, k, p + HF, rs]
                if lo < 0:
                    value = jnp.where(inside(p), value, 0.0)
                upd[slot, s, k, p + HU, rs] = value

        chunks(lo, hi, body)

    def smooth(s, slot, lo, hi):
        number = hi - lo

        @pl.loop(0, 3)
        def _(k):
            @pl.loop(0, number, unroll=number)
            def _(i):
                at = i + lo + HU
                value = taps[2] * upd[slot, s, k, at]
                value = value + taps[1] * (upd[slot, s, k, at - 1] + upd[slot, s, k, at + 1])
                value = value + taps[0] * (upd[slot, s, k, at - 2] + upd[slot, s, k, at + 2])
                hi_part, lo_part = split(value)
                stack = jnp.concatenate([hi_part, lo_part, hi_part], axis=0)
                value = jnp.dot(wrow[...], stack, preferred_element_type=jnp.float32)
                hi_part, lo_part = split(value)
                half_hi[i] = hi_part
                half_lo[i] = lo_part

            a = half_hi[0:number].reshape(number * rows, cols)
            b = half_lo[0:number].reshape(number * rows, cols)
            stack = jnp.concatenate([a, b, a], axis=1)
            value = jnp.dot(stack, wcol[...], preferred_element_type=jnp.float32)
            fld[s, k, pl.ds(lo + HF, number)] = value.reshape(number, rows, cols)

    def exchange(s, slot):
        return faces(upd.at[slot, s], upd.at[slot, s], RAD, HU, HU, (whole,),
                     upd_send.at[slot, s], upd_recv.at[slot, s])

    def mean_image(keep):
        def body(p, rs):
            images_here = [warp(s, p, rs) for s in range(count_s)]
            if keep:
                for s in range(count_s):
                    warped[s, p, rs] = images_here[s]
            total = images_here[0]
            for value in images_here[1:]:
                total = total + value
            mean[p + 1, rs] = total * (1.0 / count_s)

        chunks(0, planes, body)

    def statistics(rnd, own_count):
        def add(p, total):
            return total + mean[p + 1]

        total = jnp.sum(lax.fori_loop(0, planes, add, jnp.zeros((rows, cols), jnp.float32)))
        center = total / own_count

        def square(p, total):
            away = mean[p + 1] - center
            return total + away * away

        spread = jnp.sum(lax.fori_loop(0, planes, square, jnp.zeros((rows, cols), jnp.float32)))
        lane = lax.broadcasted_iota(jnp.int32, (8, 128), 1)
        tile[rnd] = jnp.where(lane == 0, total, jnp.where(lane == 1, spread, 0.0))
        stats[rnd, 0] = tile[rnd]
        copies = []
        for k in range(1, n):
            copy = pltpu.make_async_remote_copy(
                src_ref=tile.at[rnd], dst_ref=stats.at[rnd, k],
                send_sem=stat_send.at[rnd, k], recv_sem=stat_recv.at[rnd, k],
                device_id={"brick": lax.rem(me + k, n)}, device_id_type=MESH)
            copy.start()
            copies.append(copy)
        for copy in copies:
            copy.wait()
        every = stats[rnd]
        lanes = lax.broadcasted_iota(jnp.int32, (n, 8, 128), 2)
        rows_of = lax.broadcasted_iota(jnp.int32, (n, 8, 128), 1)
        on_sum = jnp.logical_and(lanes == 0, rows_of == 0)
        on_spread = jnp.logical_and(lanes == 1, rows_of == 0)
        count = own_count * n
        mu = jnp.sum(jnp.where(on_sum, every, 0.0)) / count
        offsets = jnp.where(on_sum, every / own_count - mu, 0.0)
        var = (jnp.sum(jnp.where(on_spread, every, 0.0)) + own_count * jnp.sum(offsets * offsets)) / count
        scale = 1.0 / jnp.sqrt(jnp.full((8, cols), var + EPS, jnp.float32))
        return mu, scale

    own_count = float(planes * rows * cols)
    out_copies = []

    load_s.wait()
    for s in range(count_s):
        shift_planes(s, 0, planes)
    load_t.wait()
    finish(tem_pair)
    gradients(-HU if LOCAL else 0, planes + (HU if LOCAL else 0))
    finish(sub_pair)
    reach = HF + 1
    for s in range(count_s):
        shift_planes(s, -reach, 0)
        shift_planes(s, planes, planes + reach)

    pairs = {}
    for rnd in range(ROUNDS):
        for step in range(ITERS):
            slot = (rnd * ITERS + step) % 2
            local = rnd == 0 and step < LOCAL
            wide = RAD * (LOCAL - step) if local else 0
            kind = "warp" if step else ("stored" if rnd else "subject")
            for s in range(count_s):
                if step:
                    settle(s)
                force(s, slot, -wide, planes + wide, kind)
                if not local:
                    pairs[s] = exchange(s, slot)
                    start(pairs[s])

            def settle(s, slot=slot, local=local, wide=wide):
                if not local:
                    finish(pairs[s])
                grow = wide - RAD if local else 0
                smooth(s, slot, -grow, planes + grow)
        for s in range(count_s):
            settle(s)
            if rnd == ROUNDS - 1:
                for k in range(3):
                    copy = pltpu.make_async_copy(
                        fld.at[s, k, pl.ds(HF, planes)], fields_out.at[k, s], out_sem.at[s, k])
                    copy.start()
                    out_copies.append(copy)
        mean_image(rnd < ROUNDS - 1)
        more = rnd < ROUNDS - 1
        if more:
            pair = faces(mean, mean, 1, 1, 1, (), mean_send, mean_recv)
            start(pair)
        mu, scale = statistics(rnd, own_count)
        if more:
            finish(pair)
        reach_mean = 1 if more else 0

        def normal(p, rs):
            value = (mean[p + 1, rs] - mu) * scale
            if more:
                value = jnp.where(inside(p), value, 0.0)
            cur[p + HT, rs] = value

        if more:
            clear(mean, (), 1, 1)
        chunks(-reach_mean, planes + reach_mean, normal)
        if more:
            gradients(0, planes)
    copy = pltpu.make_async_copy(cur.at[pl.ds(HT, planes)], atlas, load_sem.at[1])
    copy.start()
    for other in out_copies:
        other.wait()
    copy.wait()


def per_device(subjects, template):
    n = lax.axis_size("brick")
    count_s, planes, rows, cols = subjects.shape
    row_hi, row_lo = band(rows)
    col_hi, col_lo = band(cols)
    wrow = jnp.asarray(np.concatenate([row_hi, row_hi, row_lo], axis=1))
    wcol = jnp.asarray(np.concatenate([col_hi, col_hi, col_lo], axis=0))
    anywhere = pl.BlockSpec(memory_space=pl.ANY)
    in_vmem = pl.BlockSpec(memory_space=pltpu.VMEM)
    dma = pltpu.SemaphoreType.DMA
    f32 = jnp.float32
    face = (rows, cols)
    atlas, fields = pl.pallas_call(
        lambda *refs: kernel(n, *refs),
        out_shape=(jax.ShapeDtypeStruct(template.shape, f32), jax.ShapeDtypeStruct((3,) + subjects.shape, f32)),
        in_specs=[anywhere, anywhere, in_vmem, in_vmem],
        out_specs=(anywhere, anywhere),
        scratch_shapes=[
            pltpu.VMEM((9, count_s, planes + 2 * HS) + face, f32),
            pltpu.VMEM((planes + 2 * HT,) + face, f32),
            pltpu.VMEM((4, planes + 2 * HU) + face, f32),
            pltpu.VMEM((2, count_s, 3, planes + 2 * HU) + face, f32),
            pltpu.VMEM((count_s, 3, planes + 2 * HF) + face, f32),
            pltpu.VMEM((count_s, planes) + face, f32),
            pltpu.VMEM((planes + 2,) + face, f32),
            pltpu.VMEM((planes + 2 * HF,) + face, jnp.bfloat16),
            pltpu.VMEM((planes + 2 * HF,) + face, jnp.bfloat16),
            pltpu.VMEM((ROUNDS, n, 8, 128), f32),
            pltpu.VMEM((ROUNDS, 8, 128), f32),
            dma((2,)),
            dma((2, 2)), dma((2, 2)),
            dma((2, count_s, 2)), dma((2, count_s, 2)),
            dma((2,)), dma((2,)),
            dma((ROUNDS, n)), dma((ROUNDS, n)),
            dma((count_s, 3)),
        ],
        compiler_params=pltpu.CompilerParams(
            collective_id=0, has_side_effects=True, vmem_limit_bytes=60 * 1024 * 1024),
    )(subjects, template, wrow, wcol)
    return atlas, fields


def solution(mesh):
    return jax.shard_map(
        per_device,
        mesh=mesh,
        in_specs=(P("group", "brick", None, None), P(("group", "brick"), None, None)),
        out_specs=(P(("group", "brick"), None, None), P(None, "group", "brick", None, None)),
        check_vma=False,
    )
```

```python
import math

import jax
import jax.numpy as jnp
import ml_dtypes
import numpy as np
from jax import lax
from jax.experimental import pallas as pl
from jax.experimental.pallas import tpu as pltpu
from jax.sharding import PartitionSpec as P

RAD = 2
ROUNDS = 2
ITERS = 3

SIGMA = 1.5
STEP = 1.0
KAPPA = 0.5
EPS = 1e-05

LOCAL = 2
HS = max(1, RAD * LOCAL)
HT = HS + 1
HU = max(RAD, RAD * LOCAL)
HF = HU - RAD

MESH = pl.DeviceIdType.MESH


def taps_list(radius):
    raw = [math.exp(-(k * k) / (2.0 * SIGMA * SIGMA)) for k in range(-radius, radius + 1)]
    total = 0.0
    for value in raw:
        total = total + value
    return [value / total for value in raw]


def band(size):
    taps = taps_list(RAD)
    full = np.zeros((size, size), np.float64)
    for k in range(-RAD, RAD + 1):
        full += np.diag(np.full(size - abs(k), taps[k + RAD]), k)
    high = full.astype(np.float32).astype(ml_dtypes.bfloat16)
    low = (full - high.astype(np.float64)).astype(np.float32).astype(ml_dtypes.bfloat16)
    return high, low


def split(value):
    high = value.astype(jnp.bfloat16)
    low = (value - high.astype(jnp.float32)).astype(jnp.bfloat16)
    return high, low


def moved(value, axis, step):
    if step == 0:
        return value
    size = value.shape[axis]
    index = lax.broadcasted_iota(jnp.int32, value.shape, axis)
    edge = size - 1 if step > 0 else 0
    return jnp.where(index == edge, 0.0, pltpu.roll(value, (-step) % size, axis))


def kernel(n, subjects, template, wrow, wcol, atlas, fields_out,
           images, cur, grad, upd, fld, warped, mean, half_hi, half_lo, stats, tile,
           load_sem, in_send, in_recv, upd_send, upd_recv, mean_send, mean_recv,
           stat_send, stat_recv, out_sem):
    me = lax.axis_index("brick")
    count_s, planes, rows, cols = subjects.shape
    has_low, has_high = me > 0, me < n - 1
    first, last = me == 0, me == n - 1
    low, high = {"brick": me - 1}, {"brick": me + 1}
    total_planes = n * planes
    taps = taps_list(RAD)

    barrier = pltpu.get_barrier_semaphore()
    for k in range(1, n):
        pl.semaphore_signal(barrier, inc=1, device_id={"brick": lax.rem(me + k, n)}, device_id_type=MESH)
    pl.semaphore_wait(barrier, n - 1)

    def inside(p):
        place = me * planes + p
        return jnp.logical_and(place >= 0, place < total_planes)

    def faces(src, dst, halo, base_src, base_dst, lead, send, recv):
        up = pltpu.make_async_remote_copy(
            src_ref=src.at[lead + (pl.ds(base_src + planes - halo, halo),)],
            dst_ref=dst.at[lead + (pl.ds(base_dst - halo, halo),)],
            send_sem=send.at[0], recv_sem=recv.at[0], device_id=high, device_id_type=MESH)
        down = pltpu.make_async_remote_copy(
            src_ref=src.at[lead + (pl.ds(base_src, halo),)],
            dst_ref=dst.at[lead + (pl.ds(base_dst + planes, halo),)],
            send_sem=send.at[1], recv_sem=recv.at[1], device_id=low, device_id_type=MESH)
        return up, down

    def start(pair):
        pl.when(has_high)(lambda: pair[0].start())
        pl.when(has_low)(lambda: pair[1].start())

    def finish(pair):
        @pl.when(has_high)
        def _():
            pair[0].wait_send()
            pair[1].wait_recv()

        @pl.when(has_low)
        def _():
            pair[1].wait_send()
            pair[0].wait_recv()

    own = images.at[4]
    whole = slice(None)
    sub_pairs = [faces(subjects, own, HS, 0, HS, (s,), in_send.at[1 + s], in_recv.at[1 + s])
                 for s in range(count_s)]
    tem_pair = faces(template, cur, HT, 0, HT, (), in_send.at[0], in_recv.at[0])
    start(tem_pair)
    for pair in sub_pairs:
        start(pair)
    load_s = pltpu.make_async_copy(subjects, own.at[:, pl.ds(HS, planes)], load_sem.at[0])
    load_t = pltpu.make_async_copy(template, cur.at[pl.ds(HT, planes)], load_sem.at[1])
    load_s.start()
    load_t.start()

    def clear(ref, lead, halo, base):
        shape = (halo, rows, cols)

        @pl.when(first)
        def _():
            ref[lead + (pl.ds(base - halo, halo),)] = jnp.zeros(shape, jnp.float32)

        @pl.when(last)
        def _():
            ref[lead + (pl.ds(base + planes, halo),)] = jnp.zeros(shape, jnp.float32)

    clear(cur, (), HT, HT)
    for s in range(count_s):
        clear(images, (4, s), HS, HS)
        for slot in range(2):
            for k in range(3):
                clear(upd, (slot, s, k), HU, HU)

    def shift_planes(s, lo, hi):
        @pl.loop(lo + HS, hi + HS)
        def _(p):
            value = images[4, s, p]
            for c in (-1, 0, 1):
                side = moved(value, 1, c)
                for b in (-1, 0, 1):
                    if (b, c) != (0, 0):
                        images[(b + 1) * 3 + c + 1, s, p] = moved(side, 0, b)

    def gradients(lo, hi):
        @pl.loop(lo, hi)
        def _(p):
            here = cur[p + HT]
            g0 = (cur[p + HT + 1] - cur[p + HT - 1]) * 0.5
            g1 = (moved(here, 0, 1) - moved(here, 0, -1)) * 0.5
            g2 = (moved(here, 1, 1) - moved(here, 1, -1)) * 0.5
            grad[0, p + HU] = g0
            grad[1, p + HU] = g1
            grad[2, p + HU] = g2
            grad[3, p + HU] = g0 * g0 + g1 * g1 + g2 * g2 + KAPPA

    def chunks(lo, hi, body):
        per = rows // 8

        @pl.loop(0, (hi - lo) * per, unroll=4)
        def _(i):
            body(lo + i // per, pl.ds(pl.multiple_of((i % per) * 8, 8), 8))

    def warp(s, p, rs):
        u = [jnp.tanh(fld[s, k, p + HF, rs]) for k in range(3)]
        pos = [v > 0.0 for v in u]
        size = [jnp.abs(v) for v in u]

        def two(c):
            here, side = [], []
            for b in (0, 1, 2):
                where = b * 3 + c
                here.append(images[where, s, p + HS, rs])
                side.append(jnp.where(pos[0], images[where, s, p + HS + 1, rs], images[where, s, p + HS - 1, rs]))
            return (here[1], side[1], jnp.where(pos[1], here[2], here[0]), jnp.where(pos[1], side[2], side[0]))

        left, middle, right = two(0), two(1), two(2)
        beside = [jnp.where(pos[2], r, l) for r, l in zip(right, left)]
        lines = [m + size[2] * (o - m) for m, o in zip(middle, beside)]
        near = lines[0] + size[0] * (lines[1] - lines[0])
        far = lines[2] + size[0] * (lines[3] - lines[2])
        return near + size[1] * (far - near)

    def force(s, slot, lo, hi, kind):
        def body(p, rs):
            if kind == "subject":
                image = images[4, s, p + HS, rs]
            elif kind == "stored":
                image = warped[s, p, rs]
            else:
                image = warp(s, p, rs)
            diff = cur[p + HT, rs] - image
            ratio = STEP * diff / (grad[3, p + HU, rs] + diff * diff)
            for k in range(3):
                value = grad[k, p + HU, rs] * ratio
                if kind != "subject":
                    value = value + fld[s, k, p + HF, rs]
                if lo < 0:
                    value = jnp.where(inside(p), value, 0.0)
                upd[slot, s, k, p + HU, rs] = value

        chunks(lo, hi, body)

    def smooth(s, slot, lo, hi):
        number = hi - lo

        @pl.loop(0, 3)
        def _(k):
            @pl.loop(0, number, unroll=number)
            def _(i):
                at = i + lo + HU
                value = taps[2] * upd[slot, s, k, at]
                value = value + taps[1] * (upd[slot, s, k, at - 1] + upd[slot, s, k, at + 1])
                value = value + taps[0] * (upd[slot, s, k, at - 2] + upd[slot, s, k, at + 2])
                hi_part, lo_part = split(value)
                stack = jnp.concatenate([hi_part, lo_part, hi_part], axis=0)
                value = jnp.dot(wrow[...], stack, preferred_element_type=jnp.float32)
                hi_part, lo_part = split(value)
                half_hi[i] = hi_part
                half_lo[i] = lo_part

            a = half_hi[0:number].reshape(number * rows, cols)
            b = half_lo[0:number].reshape(number * rows, cols)
            stack = jnp.concatenate([a, b, a], axis=1)
            value = jnp.dot(stack, wcol[...], preferred_element_type=jnp.float32)
            fld[s, k, pl.ds(lo + HF, number)] = value.reshape(number, rows, cols)

    def exchange(s, slot):
        return faces(upd.at[slot, s], upd.at[slot, s], RAD, HU, HU, (whole,),
                     upd_send.at[slot, s], upd_recv.at[slot, s])

    def mean_image(keep):
        def body(p, rs):
            images_here = [warp(s, p, rs) for s in range(count_s)]
            if keep:
                for s in range(count_s):
                    warped[s, p, rs] = images_here[s]
            total = images_here[0]
            for value in images_here[1:]:
                total = total + value
            mean[p + 1, rs] = total * (1.0 / count_s)

        chunks(0, planes, body)

    def statistics(rnd, own_count):
        def add(p, total):
            return total + mean[p + 1]

        total = jnp.sum(lax.fori_loop(0, planes, add, jnp.zeros((rows, cols), jnp.float32)))
        center = total / own_count

        def square(p, total):
            away = mean[p + 1] - center
            return total + away * away

        spread = jnp.sum(lax.fori_loop(0, planes, square, jnp.zeros((rows, cols), jnp.float32)))
        lane = lax.broadcasted_iota(jnp.int32, (8, 128), 1)
        tile[rnd] = jnp.where(lane == 0, total, jnp.where(lane == 1, spread, 0.0))
        stats[rnd, 0] = tile[rnd]
        copies = []
        for k in range(1, n):
            copy = pltpu.make_async_remote_copy(
                src_ref=tile.at[rnd], dst_ref=stats.at[rnd, k],
                send_sem=stat_send.at[rnd, k], recv_sem=stat_recv.at[rnd, k],
                device_id={"brick": lax.rem(me + k, n)}, device_id_type=MESH)
            copy.start()
            copies.append(copy)
        for copy in copies:
            copy.wait()
        every = stats[rnd]
        lanes = lax.broadcasted_iota(jnp.int32, (n, 8, 128), 2)
        rows_of = lax.broadcasted_iota(jnp.int32, (n, 8, 128), 1)
        on_sum = jnp.logical_and(lanes == 0, rows_of == 0)
        on_spread = jnp.logical_and(lanes == 1, rows_of == 0)
        count = own_count * n
        mu = jnp.sum(jnp.where(on_sum, every, 0.0)) / count
        offsets = jnp.where(on_sum, every / own_count - mu, 0.0)
        var = (jnp.sum(jnp.where(on_spread, every, 0.0)) + own_count * jnp.sum(offsets * offsets)) / count
        scale = 1.0 / jnp.sqrt(jnp.full((8, cols), var + EPS, jnp.float32))
        return mu, scale

    own_count = float(planes * rows * cols)
    out_copies = []

    load_s.wait()
    for s in range(count_s):
        shift_planes(s, 0, planes)
    load_t.wait()
    finish(tem_pair)
    gradients(-HU if LOCAL else 0, planes + (HU if LOCAL else 0))
    reach = HF + 1
    pairs = {}

    def advance(rnd, step, s):
        slot = (rnd * ITERS + step) % 2
        force(s, slot, 0, planes, "warp" if step else ("stored" if rnd else "subject"))
        pairs[s] = exchange(s, slot)
        start(pairs[s])

    for rnd in range(ROUNDS):
        head = LOCAL if rnd == 0 else 0
        for s in range(count_s):
            if rnd == 0:
                finish(sub_pairs[s])
                shift_planes(s, -reach, 0)
                shift_planes(s, planes, planes + reach)
            for step in range(head):
                wide = RAD * (LOCAL - step)
                force(s, (LOCAL + 1) % 2, -wide, planes + wide, "warp" if step else "subject")
                smooth(s, (LOCAL + 1) % 2, RAD - wide, planes + wide - RAD)
            if head < ITERS:
                advance(rnd, head, s)
        for step in range(head + 1, ITERS):
            for s in range(count_s):
                finish(pairs[s])
                smooth(s, (rnd * ITERS + step - 1) % 2, 0, planes)
                advance(rnd, step, s)
        for s in range(count_s):
            if head < ITERS:
                finish(pairs[s])
                smooth(s, (rnd * ITERS + ITERS - 1) % 2, 0, planes)
            if rnd == ROUNDS - 1:
                for k in range(3):
                    copy = pltpu.make_async_copy(
                        fld.at[s, k, pl.ds(HF, planes)], fields_out.at[k, s], out_sem.at[s, k])
                    copy.start()
                    out_copies.append(copy)
        mean_image(rnd < ROUNDS - 1)
        more = rnd < ROUNDS - 1
        if more:
            pair = faces(mean, mean, 1, 1, 1, (), mean_send, mean_recv)
            start(pair)
        mu, scale = statistics(rnd, own_count)
        if more:
            finish(pair)
        reach_mean = 1 if more else 0

        def normal(p, rs):
            value = (mean[p + 1, rs] - mu) * scale
            if more:
                value = jnp.where(inside(p), value, 0.0)
            cur[p + HT, rs] = value

        if more:
            clear(mean, (), 1, 1)
        chunks(-reach_mean, planes + reach_mean, normal)
        if more:
            gradients(0, planes)
    copy = pltpu.make_async_copy(cur.at[pl.ds(HT, planes)], atlas, load_sem.at[1])
    copy.start()
    for other in out_copies:
        other.wait()
    copy.wait()


def per_device(subjects, template):
    n = lax.axis_size("brick")
    count_s, planes, rows, cols = subjects.shape
    row_hi, row_lo = band(rows)
    col_hi, col_lo = band(cols)
    wrow = jnp.asarray(np.concatenate([row_hi, row_hi, row_lo], axis=1))
    wcol = jnp.asarray(np.concatenate([col_hi, col_hi, col_lo], axis=0))
    anywhere = pl.BlockSpec(memory_space=pl.ANY)
    in_vmem = pl.BlockSpec(memory_space=pltpu.VMEM)
    dma = pltpu.SemaphoreType.DMA
    f32 = jnp.float32
    face = (rows, cols)
    atlas, fields = pl.pallas_call(
        lambda *refs: kernel(n, *refs),
        out_shape=(jax.ShapeDtypeStruct(template.shape, f32), jax.ShapeDtypeStruct((3,) + subjects.shape, f32)),
        in_specs=[anywhere, anywhere, in_vmem, in_vmem],
        out_specs=(anywhere, anywhere),
        scratch_shapes=[
            pltpu.VMEM((9, count_s, planes + 2 * HS) + face, f32),
            pltpu.VMEM((planes + 2 * HT,) + face, f32),
            pltpu.VMEM((4, planes + 2 * HU) + face, f32),
            pltpu.VMEM((2, count_s, 3, planes + 2 * HU) + face, f32),
            pltpu.VMEM((count_s, 3, planes + 2 * HF) + face, f32),
            pltpu.VMEM((count_s, planes) + face, f32),
            pltpu.VMEM((planes + 2,) + face, f32),
            pltpu.VMEM((planes + 2 * HF,) + face, jnp.bfloat16),
            pltpu.VMEM((planes + 2 * HF,) + face, jnp.bfloat16),
            pltpu.VMEM((ROUNDS, n, 8, 128), f32),
            pltpu.VMEM((ROUNDS, 8, 128), f32),
            dma((2,)),
            dma((1 + count_s, 2)), dma((1 + count_s, 2)),
            dma((2, count_s, 2)), dma((2, count_s, 2)),
            dma((2,)), dma((2,)),
            dma((ROUNDS, n)), dma((ROUNDS, n)),
            dma((count_s, 3)),
        ],
        compiler_params=pltpu.CompilerParams(
            collective_id=0, has_side_effects=True, vmem_limit_bytes=60 * 1024 * 1024),
    )(subjects, template, wrow, wcol)
    return atlas, fields


def solution(mesh):
    return jax.shard_map(
        per_device,
        mesh=mesh,
        in_specs=(P("group", "brick", None, None), P(("group", "brick"), None, None)),
        out_specs=(P(("group", "brick"), None, None), P(None, "group", "brick", None, None)),
        check_vma=False,
    )
```

```python
import math

import jax
import jax.numpy as jnp
import ml_dtypes
import numpy as np
from jax import lax
from jax.experimental import pallas as pl
from jax.experimental.pallas import tpu as pltpu
from jax.sharding import PartitionSpec as P

RAD = 2
ROUNDS = 2
ITERS = 3

SIGMA = 1.5
STEP = 1.0
KAPPA = 0.5
EPS = 1e-05

LOCAL = 2
HS = max(1, RAD * LOCAL)
HT = HS + 1
HU = max(RAD, RAD * LOCAL)
HF = HU - RAD

MESH = pl.DeviceIdType.MESH


def taps_list(radius):
    raw = [math.exp(-(k * k) / (2.0 * SIGMA * SIGMA)) for k in range(-radius, radius + 1)]
    total = 0.0
    for value in raw:
        total = total + value
    return [value / total for value in raw]


def band(size):
    taps = taps_list(RAD)
    full = np.zeros((size, size), np.float64)
    for k in range(-RAD, RAD + 1):
        full += np.diag(np.full(size - abs(k), taps[k + RAD]), k)
    high = full.astype(np.float32).astype(ml_dtypes.bfloat16)
    low = (full - high.astype(np.float64)).astype(np.float32).astype(ml_dtypes.bfloat16)
    return high, low


def split(value):
    high = value.astype(jnp.bfloat16)
    low = (value - high.astype(jnp.float32)).astype(jnp.bfloat16)
    return high, low


def moved(value, axis, step):
    if step == 0:
        return value
    size = value.shape[axis]
    index = lax.broadcasted_iota(jnp.int32, value.shape, axis)
    edge = size - 1 if step > 0 else 0
    return jnp.where(index == edge, 0.0, pltpu.roll(value, (-step) % size, axis))


def kernel(n, subjects, template, wrow, wcol, atlas, fields_out,
           images, cur, grad, upd, fld, warped, mean, half_hi, half_lo, stats, tile,
           load_sem, in_send, in_recv, upd_send, upd_recv, mean_send, mean_recv,
           stat_send, stat_recv, out_sem):
    me = lax.axis_index("brick")
    count_s, planes, rows, cols = subjects.shape
    has_low, has_high = me > 0, me < n - 1
    first, last = me == 0, me == n - 1
    low, high = {"brick": me - 1}, {"brick": me + 1}
    total_planes = n * planes
    taps = taps_list(RAD)

    barrier = pltpu.get_barrier_semaphore()
    for k in range(1, n):
        pl.semaphore_signal(barrier, inc=1, device_id={"brick": lax.rem(me + k, n)}, device_id_type=MESH)
    pl.semaphore_wait(barrier, n - 1)

    def inside(p):
        place = me * planes + p
        return jnp.logical_and(place >= 0, place < total_planes)

    def faces(src, dst, halo, base_src, base_dst, lead, send, recv):
        up = pltpu.make_async_remote_copy(
            src_ref=src.at[lead + (pl.ds(base_src + planes - halo, halo),)],
            dst_ref=dst.at[lead + (pl.ds(base_dst - halo, halo),)],
            send_sem=send.at[0], recv_sem=recv.at[0], device_id=high, device_id_type=MESH)
        down = pltpu.make_async_remote_copy(
            src_ref=src.at[lead + (pl.ds(base_src, halo),)],
            dst_ref=dst.at[lead + (pl.ds(base_dst + planes, halo),)],
            send_sem=send.at[1], recv_sem=recv.at[1], device_id=low, device_id_type=MESH)
        return up, down

    def start(pair):
        pl.when(has_high)(lambda: pair[0].start())
        pl.when(has_low)(lambda: pair[1].start())

    def finish(pair):
        @pl.when(has_high)
        def _():
            pair[0].wait_send()
            pair[1].wait_recv()

        @pl.when(has_low)
        def _():
            pair[1].wait_send()
            pair[0].wait_recv()

    own = images.at[4]
    whole = slice(None)
    sub_pairs = [faces(subjects, own, HS, 0, HS, (s,), in_send.at[1 + s], in_recv.at[1 + s])
                 for s in range(count_s)]
    tem_pair = faces(template, cur, HT, 0, HT, (), in_send.at[0], in_recv.at[0])
    start(tem_pair)
    for pair in sub_pairs:
        start(pair)
    load_s = pltpu.make_async_copy(subjects, own.at[:, pl.ds(HS, planes)], load_sem.at[0])
    load_t = pltpu.make_async_copy(template, cur.at[pl.ds(HT, planes)], load_sem.at[1])
    load_s.start()
    load_t.start()

    def clear(ref, lead, halo, base):
        shape = (halo, rows, cols)

        @pl.when(first)
        def _():
            ref[lead + (pl.ds(base - halo, halo),)] = jnp.zeros(shape, jnp.float32)

        @pl.when(last)
        def _():
            ref[lead + (pl.ds(base + planes, halo),)] = jnp.zeros(shape, jnp.float32)

    clear(cur, (), HT, HT)
    for s in range(count_s):
        clear(images, (4, s), HS, HS)
        for slot in range(2):
            for k in range(3):
                clear(upd, (slot, s, k), HU, HU)

    def shift_planes(s, lo, hi):
        @pl.loop(lo + HS, hi + HS)
        def _(p):
            value = images[4, s, p]
            for c in (-1, 0, 1):
                side = moved(value, 1, c)
                for b in (-1, 0, 1):
                    if (b, c) != (0, 0):
                        images[(b + 1) * 3 + c + 1, s, p] = moved(side, 0, b)

    def gradients(lo, hi):
        @pl.loop(lo, hi)
        def _(p):
            here = cur[p + HT]
            g0 = (cur[p + HT + 1] - cur[p + HT - 1]) * 0.5
            g1 = (moved(here, 0, 1) - moved(here, 0, -1)) * 0.5
            g2 = (moved(here, 1, 1) - moved(here, 1, -1)) * 0.5
            grad[0, p + HU] = g0
            grad[1, p + HU] = g1
            grad[2, p + HU] = g2
            grad[3, p + HU] = g0 * g0 + g1 * g1 + g2 * g2 + KAPPA

    def chunks(lo, hi, body):
        per = rows // 8

        @pl.loop(0, (hi - lo) * per, unroll=4)
        def _(i):
            body(lo + i // per, pl.ds(pl.multiple_of((i % per) * 8, 8), 8))

    def warp(s, p, rs):
        u = [jnp.tanh(fld[s, k, p + HF, rs]) for k in range(3)]
        pos = [v > 0.0 for v in u]
        size = [jnp.abs(v) for v in u]

        def two(c):
            here, side = [], []
            for b in (0, 1, 2):
                where = b * 3 + c
                here.append(images[where, s, p + HS, rs])
                side.append(jnp.where(pos[0], images[where, s, p + HS + 1, rs], images[where, s, p + HS - 1, rs]))
            return (here[1], side[1], jnp.where(pos[1], here[2], here[0]), jnp.where(pos[1], side[2], side[0]))

        left, middle, right = two(0), two(1), two(2)
        beside = [jnp.where(pos[2], r, l) for r, l in zip(right, left)]
        lines = [m + size[2] * (o - m) for m, o in zip(middle, beside)]
        near = lines[0] + size[0] * (lines[1] - lines[0])
        far = lines[2] + size[0] * (lines[3] - lines[2])
        return near + size[1] * (far - near)

    def force(s, slot, lo, hi, kind):
        def body(p, rs):
            if kind == "subject":
                image = images[4, s, p + HS, rs]
            elif kind == "stored":
                image = warped[s, p, rs]
            else:
                image = warp(s, p, rs)
            diff = cur[p + HT, rs] - image
            ratio = STEP * diff / (grad[3, p + HU, rs] + diff * diff)
            for k in range(3):
                value = grad[k, p + HU, rs] * ratio
                if kind != "subject":
                    value = value + fld[s, k, p + HF, rs]
                if lo < 0:
                    value = jnp.where(inside(p), value, 0.0)
                upd[slot, s, k, p + HU, rs] = value

        chunks(lo, hi, body)

    def smooth(s, slot, lo, hi):
        number = hi - lo

        @pl.loop(0, 3)
        def _(k):
            @pl.loop(0, number, unroll=number)
            def _(i):
                at = i + lo + HU
                value = taps[2] * upd[slot, s, k, at]
                value = value + taps[1] * (upd[slot, s, k, at - 1] + upd[slot, s, k, at + 1])
                value = value + taps[0] * (upd[slot, s, k, at - 2] + upd[slot, s, k, at + 2])
                hi_part, lo_part = split(value)
                stack = jnp.concatenate([hi_part, lo_part, hi_part], axis=0)
                value = jnp.dot(wrow[...], stack, preferred_element_type=jnp.float32)
                hi_part, lo_part = split(value)
                half_hi[i] = hi_part
                half_lo[i] = lo_part

            a = half_hi[0:number].reshape(number * rows, cols)
            b = half_lo[0:number].reshape(number * rows, cols)
            stack = jnp.concatenate([a, b, a], axis=1)
            value = jnp.dot(stack, wcol[...], preferred_element_type=jnp.float32)
            fld[s, k, pl.ds(lo + HF, number)] = value.reshape(number, rows, cols)

    def exchange(s, slot):
        return faces(upd.at[slot, s], upd.at[slot, s], RAD, HU, HU, (whole,),
                     upd_send.at[slot, s], upd_recv.at[slot, s])

    def mean_image(keep):
        def body(p, rs):
            images_here = [warp(s, p, rs) for s in range(count_s)]
            if keep:
                for s in range(count_s):
                    warped[s, p, rs] = images_here[s]
            total = images_here[0]
            for value in images_here[1:]:
                total = total + value
            mean[p + 1, rs] = total * (1.0 / count_s)

        chunks(0, planes, body)

    def statistics(rnd, own_count):
        def add(p, total):
            return total + mean[p + 1]

        total = jnp.sum(lax.fori_loop(0, planes, add, jnp.zeros((rows, cols), jnp.float32)))
        center = total / own_count

        def square(p, total):
            away = mean[p + 1] - center
            return total + away * away

        spread = jnp.sum(lax.fori_loop(0, planes, square, jnp.zeros((rows, cols), jnp.float32)))
        lane = lax.broadcasted_iota(jnp.int32, (8, 128), 1)
        tile[rnd] = jnp.where(lane == 0, total, jnp.where(lane == 1, spread, 0.0))
        stats[rnd, 0] = tile[rnd]
        copies = []
        for k in range(1, n):
            copy = pltpu.make_async_remote_copy(
                src_ref=tile.at[rnd], dst_ref=stats.at[rnd, k],
                send_sem=stat_send.at[rnd, k], recv_sem=stat_recv.at[rnd, k],
                device_id={"brick": lax.rem(me + k, n)}, device_id_type=MESH)
            copy.start()
            copies.append(copy)
        for copy in copies:
            copy.wait()
        every = stats[rnd]
        lanes = lax.broadcasted_iota(jnp.int32, (n, 8, 128), 2)
        rows_of = lax.broadcasted_iota(jnp.int32, (n, 8, 128), 1)
        on_sum = jnp.logical_and(lanes == 0, rows_of == 0)
        on_spread = jnp.logical_and(lanes == 1, rows_of == 0)
        count = own_count * n
        mu = jnp.sum(jnp.where(on_sum, every, 0.0)) / count
        offsets = jnp.where(on_sum, every / own_count - mu, 0.0)
        var = (jnp.sum(jnp.where(on_spread, every, 0.0)) + own_count * jnp.sum(offsets * offsets)) / count
        scale = 1.0 / jnp.sqrt(jnp.full((8, cols), var + EPS, jnp.float32))
        return mu, scale

    own_count = float(planes * rows * cols)
    out_copies = []

    load_s.wait()
    for s in range(count_s):
        shift_planes(s, 0, planes)
    load_t.wait()
    finish(tem_pair)
    gradients(-HU if LOCAL else 0, planes + (HU if LOCAL else 0))
    reach = HF + 1
    pairs = {}

    def advance(rnd, step, s):
        slot = (rnd * ITERS + step) % 2
        kind = "warp" if step else ("stored" if rnd else "subject")
        force(s, slot, 0, RAD, kind)
        force(s, slot, planes - RAD, planes, kind)
        pairs[s] = exchange(s, slot)
        start(pairs[s])
        force(s, slot, RAD, planes - RAD, kind)

    for rnd in range(ROUNDS):
        head = LOCAL if rnd == 0 else 0
        for s in range(count_s):
            if rnd == 0:
                finish(sub_pairs[s])
                shift_planes(s, -reach, 0)
                shift_planes(s, planes, planes + reach)
            for step in range(head):
                wide = RAD * (LOCAL - step)
                force(s, (LOCAL + 1) % 2, -wide, planes + wide, "warp" if step else "subject")
                smooth(s, (LOCAL + 1) % 2, RAD - wide, planes + wide - RAD)
            if head < ITERS:
                advance(rnd, head, s)
        for step in range(head + 1, ITERS):
            for s in range(count_s):
                finish(pairs[s])
                smooth(s, (rnd * ITERS + step - 1) % 2, 0, planes)
                advance(rnd, step, s)
        for s in range(count_s):
            if head < ITERS:
                finish(pairs[s])
                smooth(s, (rnd * ITERS + ITERS - 1) % 2, 0, planes)
            if rnd == ROUNDS - 1:
                for k in range(3):
                    copy = pltpu.make_async_copy(
                        fld.at[s, k, pl.ds(HF, planes)], fields_out.at[k, s], out_sem.at[s, k])
                    copy.start()
                    out_copies.append(copy)
        mean_image(rnd < ROUNDS - 1)
        more = rnd < ROUNDS - 1
        if more:
            pair = faces(mean, mean, 1, 1, 1, (), mean_send, mean_recv)
            start(pair)
        mu, scale = statistics(rnd, own_count)
        if more:
            finish(pair)
        reach_mean = 1 if more else 0

        def normal(p, rs):
            value = (mean[p + 1, rs] - mu) * scale
            if more:
                value = jnp.where(inside(p), value, 0.0)
            cur[p + HT, rs] = value

        if more:
            clear(mean, (), 1, 1)
        chunks(-reach_mean, planes + reach_mean, normal)
        if more:
            gradients(0, planes)
    copy = pltpu.make_async_copy(cur.at[pl.ds(HT, planes)], atlas, load_sem.at[1])
    copy.start()
    for other in out_copies:
        other.wait()
    copy.wait()


def per_device(subjects, template):
    n = lax.axis_size("brick")
    count_s, planes, rows, cols = subjects.shape
    row_hi, row_lo = band(rows)
    col_hi, col_lo = band(cols)
    wrow = jnp.asarray(np.concatenate([row_hi, row_hi, row_lo], axis=1))
    wcol = jnp.asarray(np.concatenate([col_hi, col_hi, col_lo], axis=0))
    anywhere = pl.BlockSpec(memory_space=pl.ANY)
    in_vmem = pl.BlockSpec(memory_space=pltpu.VMEM)
    dma = pltpu.SemaphoreType.DMA
    f32 = jnp.float32
    face = (rows, cols)
    atlas, fields = pl.pallas_call(
        lambda *refs: kernel(n, *refs),
        out_shape=(jax.ShapeDtypeStruct(template.shape, f32), jax.ShapeDtypeStruct((3,) + subjects.shape, f32)),
        in_specs=[anywhere, anywhere, in_vmem, in_vmem],
        out_specs=(anywhere, anywhere),
        scratch_shapes=[
            pltpu.VMEM((9, count_s, planes + 2 * HS) + face, f32),
            pltpu.VMEM((planes + 2 * HT,) + face, f32),
            pltpu.VMEM((4, planes + 2 * HU) + face, f32),
            pltpu.VMEM((2, count_s, 3, planes + 2 * HU) + face, f32),
            pltpu.VMEM((count_s, 3, planes + 2 * HF) + face, f32),
            pltpu.VMEM((count_s, planes) + face, f32),
            pltpu.VMEM((planes + 2,) + face, f32),
            pltpu.VMEM((planes + 2 * HF,) + face, jnp.bfloat16),
            pltpu.VMEM((planes + 2 * HF,) + face, jnp.bfloat16),
            pltpu.VMEM((ROUNDS, n, 8, 128), f32),
            pltpu.VMEM((ROUNDS, 8, 128), f32),
            dma((2,)),
            dma((1 + count_s, 2)), dma((1 + count_s, 2)),
            dma((2, count_s, 2)), dma((2, count_s, 2)),
            dma((2,)), dma((2,)),
            dma((ROUNDS, n)), dma((ROUNDS, n)),
            dma((count_s, 3)),
        ],
        compiler_params=pltpu.CompilerParams(
            collective_id=0, has_side_effects=True, vmem_limit_bytes=60 * 1024 * 1024),
    )(subjects, template, wrow, wcol)
    return atlas, fields


def solution(mesh):
    return jax.shard_map(
        per_device,
        mesh=mesh,
        in_specs=(P("group", "brick", None, None), P(("group", "brick"), None, None)),
        out_specs=(P(("group", "brick"), None, None), P(None, "group", "brick", None, None)),
        check_vma=False,
    )
```
